256 devices in a mesh: grp: 4 (over x), mem: 64 (over z, y, core).
Axes of the slice: x: 4, y: 4, z: 8, core: 2. Of those that a mesh axis runs over, the one named last changes fastest.
Arguments:
- bank: bfloat16 [196608, 1024], P(('grp', 'mem')), may hold values from -1 to 1
- pattern: int32 [1536, 384], P(('grp', 'mem')), may hold values from 0 to 1, as said below
- pair_list: int32 [256, 4, 4], P(('grp', 'mem')), may hold values from 0 to 5, as said below
- pair_count: int32 [256, 4], P(('grp', 'mem')), may hold values from 0 to 4, as said below
Outputs:
- coarse_best: float32 [196608], P(('grp', 'mem'))
- fine_best: float32 [196608], P(('grp', 'mem'))
The draws below stay inside these ranges and needn't reach their ends.
Inputs may be any that keep to these rules, and one draw needn't show every extreme that they name: pattern is symmetric inside each group's 384 x 384 block and 1 on its diagonal. `pair_list`: values in slots at or beyond pair_count, and in a device's own group, are not read; a block may be listed more than once. `pair_count`: zero for a device's own group; every device has a live slot; for one member index drawn from the seed, every device of that index has 4 live slots toward every other group.
All inputs are finite; a program needn't handle non-finite values.
Results may differ from the reference program's by a relative error of at most 0.0003.
Values may be sent and summed in bfloat16 or wider, within the bound.
A program may use at most 64 MiB of HBM per device.

```python
import jax
import jax.numpy as jnp
from jax import lax

D = 1024
PREF = 64
BLK = 128
CAP = 4
ROWS_DEV = 768
ROWS = 196608
GB = 384
N_GRP = 4
N_MEM = 64


def draw_pattern(key, part):
    key = jax.random.fold_in(key, 11)
    bits = jax.random.randint(key, (N_GRP, GB, GB), 0, 2)
    row_ids = jnp.arange(GB)[:, None]
    col_ids = jnp.arange(GB)[None, :]
    sym = jnp.where(row_ids <= col_ids, bits, jnp.swapaxes(bits, 1, 2))
    sym = jnp.where(row_ids == col_ids, 1, sym)
    return sym.reshape(N_GRP * GB, GB).astype(jnp.int32)


def draw_pair_list(key, part):
    key = jax.random.fold_in(key, 23)
    return jax.random.randint(key, (N_GRP * N_MEM, N_GRP, CAP), 0, ROWS_DEV // BLK).astype(jnp.int32)


def draw_pair_count(key, part):
    key = jax.random.fold_in(key, 37)
    first, second, third = jax.random.split(key, 3)
    devices = N_GRP * N_MEM
    counts = jax.random.randint(first, (devices, N_GRP), 0, CAP + 1)
    busy = jax.random.randint(second, (devices, 1), 0, 4) == 0
    counts = jnp.where(busy, CAP, counts)
    chosen = jax.random.randint(third, (), 0, N_MEM)
    device_ids = jnp.arange(devices)
    counts = jnp.where((device_ids % N_MEM == chosen)[:, None], CAP, counts)
    own = device_ids // N_MEM
    groups = jnp.arange(N_GRP)[None, :]
    nextg = ((own + 1) % N_GRP)[:, None]
    counts = jnp.where(groups == nextg, jnp.maximum(counts, 1), counts)
    counts = jnp.where(groups == own[:, None], 0, counts)
    return counts.astype(jnp.int32)


def level_of(stream_key, shape, pieces, smallest, top_value):
    factor_of = 1.0
    for axis_at, shards_of in pieces:
        heights = jax.random.uniform(jax.random.fold_in(jax.random.fold_in(stream_key, 6), axis_at), (shards_of,), jnp.float32, smallest / len(pieces), top_value / len(pieces))
        factor_of = factor_of * jnp.repeat(jnp.exp(heights), shape[axis_at] // shards_of).reshape((-1,) + (1,) * (len(shape) - 1 - axis_at))
    return factor_of


def normal_values(rng, shape, deviation, limit, shards=(), kind=jnp.bfloat16):
    array = jax.random.normal(rng, shape, jnp.float32) * deviation
    if len(shards) > 0:
        array = level_of(rng, shape, shards, -0.22, 0.18) * array
    return jnp.clip(array, min=-limit, max=limit).astype(kind)


def setup_inputs(seed: int = 0) -> dict:
    streams_of = jax.random.split(jax.random.key(seed), 5)
    bank = normal_values(streams_of[0], (ROWS, D), 0.177, 1.0, ((0, 256),))
    pattern = draw_pattern(jax.random.fold_in(streams_of[4], 71), 0)
    pair_list = draw_pair_list(jax.random.fold_in(streams_of[4], 71), 0)
    pair_count = draw_pair_count(jax.random.fold_in(streams_of[4], 71), 0)
    return {"bank": bank, "pattern": pattern, "pair_list": pair_list, "pair_count": pair_count}


NEG = -1.0e30


def reference(bank, pattern, pair_list, pair_count):
    group_rows = ROWS_DEV * N_MEM
    total_rows = bank.shape[0]
    prefix = bank[:, :PREF].astype(jnp.float32).reshape(N_GRP, group_rows, PREF)
    patt = pattern.reshape(N_GRP, GB, GB)
    per_group = group_rows // 256

    def coarse_block(q):
        group = q // per_group
        local = q % per_group
        grp_pref = lax.dynamic_index_in_dim(prefix, group, 0, keepdims=False)
        grp_patt = lax.dynamic_index_in_dim(patt, group, 0, keepdims=False)
        mine = lax.dynamic_slice_in_dim(grp_pref, (local * 256).astype(jnp.int32), 256, 0)
        scores = jnp.dot(mine, grp_pref.T, precision=lax.Precision.HIGHEST)
        prow = lax.dynamic_slice_in_dim(grp_patt, (local * (256 // BLK)).astype(jnp.int32), 256 // BLK, 0)
        keep = jnp.broadcast_to(prow[:, None, :, None] > 0, (256 // BLK, BLK, GB, BLK)).reshape(256, group_rows)
        row_ids = local * 256 + jnp.arange(256, dtype=jnp.int32)
        col_ids = jnp.arange(group_rows, dtype=jnp.int32)
        keep = keep & (row_ids[:, None] != col_ids[None, :])
        return jnp.max(jnp.where(keep, scores, NEG), axis=1)

    coarse = lax.map(coarse_block, jnp.arange(N_GRP * per_group, dtype=jnp.int32)).reshape(total_rows)

    def fine_step(carry, device):
        own_group = device // N_MEM
        member = device % N_MEM
        local = lax.dynamic_slice_in_dim(bank, (device * ROWS_DEV).astype(jnp.int32), ROWS_DEV, 0).astype(jnp.float32)
        ids = pair_list[device]
        counts = pair_count[device]
        owners = jnp.arange(N_GRP, dtype=jnp.int32) * N_MEM + member
        starts = (owners[:, None] * ROWS_DEV + ids * BLK).reshape(-1).astype(jnp.int32)
        blocks = jax.vmap(lambda s: lax.dynamic_slice_in_dim(bank, s, BLK, 0))(starts).astype(jnp.float32)
        scores = jnp.einsum("rd,skd->srk", local, blocks, precision=lax.Precision.HIGHEST)
        valid = (jnp.arange(CAP, dtype=jnp.int32)[None, :] < counts[:, None]) & (jnp.arange(N_GRP, dtype=jnp.int32)[:, None] != own_group)
        masked = jnp.where(valid.reshape(-1)[:, None, None], scores, NEG)
        row_best = jnp.max(masked, axis=(0, 2))
        col_best = jnp.max(masked, axis=1)
        start_own = (device * ROWS_DEV).astype(jnp.int32)
        current = lax.dynamic_slice_in_dim(carry, start_own, ROWS_DEV, 0)
        carry = lax.dynamic_update_slice_in_dim(carry, jnp.maximum(current, row_best), start_own, 0)
        index = (starts[:, None] + jnp.arange(BLK, dtype=jnp.int32)[None, :]).reshape(-1)
        carry = carry.at[index].max(col_best.reshape(-1))
        return carry, None

    fine, _ = lax.scan(fine_step, jnp.full((total_rows,), NEG, jnp.float32), jnp.arange(N_GRP * N_MEM, dtype=jnp.int32))
    return coarse, fine
```

```python
import functools

import jax
import jax.numpy as jnp
from jax import lax
from jax.experimental import pallas as pl
from jax.experimental.pallas import tpu as pltpu
from jax.sharding import PartitionSpec as P

PREF = 64
BLK = 128
NEG = -1e30
MESH = pl.DeviceIdType.MESH
COVERS = {64: (0, 1, 63, 58, 15, 41, 13, 4, 33), 4: (0, 1, 2)}


def dot_nt(a, b):
    return lax.dot_general(a, b, (((1,), (1,)), ((), ())), preferred_element_type=jnp.float32)


def kernel(
    cover, groups, members,
    bank, patt, plist, pcount,
    coarse, fine,
    own, pre, prev, lbuf, lsend, recv, lhs, rhs, racc, cacc, cret,
    pattpad, sel, ids, ids_s, f_own, f_prev, f_l, r2s, r1, r2,
    loc_sem, id_send, id_recv, c_send, c_recv, a_send, a_recv, l_send, l_recv, b_send, b_recv, r_send, r_recv,
):
    g = lax.axis_index("grp")
    m = lax.axis_index("mem")
    core = lax.rem(m, 2)
    nxt = lax.rem(g + 1 + 2 * core, groups)
    prv = lax.rem(g + 3 - 2 * core, groups)
    opp = lax.rem(g + 2, groups)
    slots = len(cover)
    rows = own.shape[0]
    half = rows // 2
    blocks = rows // BLK
    cap = lbuf.shape[0] // BLK
    to_user = [None] + [lax.rem(m + members - d, members) for d in cover[1:]]
    to_owner = [None] + [lax.rem(m + d, members) for d in cover[1:]]

    pre_copy = pltpu.make_async_copy(bank.at[:, pl.ds(0, 128)], pre, loc_sem.at[0])
    pre_copy.start()
    own_copy = pltpu.make_async_copy(bank, own, loc_sem.at[1])
    own_copy.start()

    barrier = pltpu.get_barrier_semaphore()
    for other in (nxt, prv, opp):
        pl.semaphore_signal(barrier, inc=1, device_id=(other, m), device_id_type=MESH)
    for k in range(1, slots):
        for other in (to_user[k], to_owner[k]):
            pl.semaphore_signal(barrier, inc=1, device_id=(g, other), device_id_type=MESH)

    lane = lax.broadcasted_iota(jnp.int32, (1, 128), 1)
    low = (lane < PREF).astype(jnp.float32)

    ids[0] = jnp.zeros((8, 128), jnp.int32)
    ids[0, 0:4, 0:4] = plist[0]
    ids[0, 4:5, 0:4] = pcount[...]
    pattpad[...] = jnp.zeros_like(pattpad)
    pattpad[0:blocks, :] = patt[...]
    for t in range(3):
        recv[0, half + 16 * t : half + 16 * t + 16, :] = (
            pattpad[:, 128 * t : 128 * t + 128].astype(jnp.float32).astype(jnp.bfloat16)
        )
    pre_copy.wait()
    recv[0, 0:half, :] = (
        pre[0:half, :].astype(jnp.float32) * low
        + pltpu.roll(pre[half:rows, :].astype(jnp.float32) * low, PREF, 1)
    ).astype(jnp.bfloat16)

    pl.semaphore_wait(barrier, 3 + 2 * (slots - 1))

    def remote(src, dst, send, rcv, where):
        copy = pltpu.make_async_remote_copy(
            src_ref=src, dst_ref=dst, send_sem=send, recv_sem=rcv, device_id=where, device_id_type=MESH
        )
        copy.start()
        return copy

    id_copies = [
        remote(ids.at[0], ids.at[1], id_send.at[0], id_recv.at[0], (nxt, m)),
        remote(ids.at[0], ids.at[2], id_send.at[1], id_recv.at[1], (opp, m)),
    ]
    c_copies = [None] + [
        remote(recv.at[0], recv.at[k], c_send.at[k], c_recv.at[k], (g, to_user[k])) for k in range(1, slots)
    ]
    a_copies = []
    for a in range(blocks):
        part = pl.ds(BLK * a, BLK)
        a_copies.append(remote(bank.at[part, :], prev.at[part, :], a_send.at[a], a_recv.at[a], (nxt, m)))

    column = jnp.full((1, 128), -1, jnp.int32)
    for k in range(slots):
        first = PREF + blocks * k
        member = m if k == 0 else to_owner[k]
        column = jnp.where((lane >= first) & (lane < first + blocks), blocks * member + lane - first, column)
    row_id = lax.broadcasted_iota(jnp.int32, sel.shape, 0)
    sel[...] = (row_id == column).astype(jnp.float32).astype(jnp.bfloat16)
    in_mask = ((lane >= PREF) & (lane < PREF + blocks * slots)).astype(jnp.float32)

    def build(k):
        bias = jnp.zeros((16, 128), jnp.float32)
        for t in range(3):
            bias = bias + jnp.dot(
                recv[k, half + 16 * t : half + 16 * t + 16, :],
                sel[128 * t : 128 * t + 128, :],
                preferred_element_type=jnp.float32,
            )
        bias = (bias - 1.0) * (-NEG) * in_mask
        for b in range(blocks):
            at = BLK * (b % (blocks // 2))
            part = recv[k, at : at + BLK, :].astype(jnp.float32)
            if b >= blocks // 2:
                part = pltpu.roll(part, PREF, 1)
            part = part * low
            hot = (lane == PREF + blocks * k + b).astype(jnp.float32)
            lhs[k, BLK * b : BLK * b + BLK, :] = (part + hot).astype(jnp.bfloat16)
            rhs[k, BLK * b : BLK * b + BLK, :] = (part + bias[b : b + 1, :]).astype(jnp.bfloat16)

    racc[...] = jnp.full_like(racc, NEG)
    cacc[...] = jnp.full_like(cacc, NEG)
    f_own[...] = jnp.full_like(f_own, NEG)
    f_prev[...] = jnp.full_like(f_prev, NEG)
    f_l[...] = jnp.full_like(f_l, NEG)

    own_copy.wait()
    for copy in id_copies:
        copy.wait_recv()
    id_local = pltpu.make_async_copy(ids, ids_s, loc_sem.at[2])
    id_local.start()
    id_local.wait()
    l_copies = []
    for j in range(cap):
        block = ids_s[2, g, j]
        picked = own[0:BLK, :]
        for b in range(1, blocks):
            picked = lax.select(block == b, own[BLK * b : BLK * b + BLK, :], picked)
        lsend[BLK * j : BLK * j + BLK, :] = picked
        part = pl.ds(BLK * j, BLK)
        l_copies.append(remote(lsend.at[part, :], lbuf.at[part, :], l_send.at[j], l_recv.at[j], (prv, m)))

    build(0)
    diag = jnp.where(
        lax.broadcasted_iota(jnp.int32, (BLK, BLK), 0) == lax.broadcasted_iota(jnp.int32, (BLK, BLK), 1), NEG, 0.0
    )

    for c in range(blocks):
        part = slice(BLK * c, BLK * c + BLK)
        s = dot_nt(lhs[0], rhs[0, part, :])
        for b in range(blocks):
            at = slice(BLK * b, BLK * b + BLK)
            x = s[at, :]
            if b == c:
                x = x + diag
            racc[0, at, :] = jnp.maximum(racc[0, at, :], x)

    def pair(a, b):
        for n in range(0, rows, 256):
            s = dot_nt(lhs[a], rhs[b, n : n + 256, :])
            racc[a] = jnp.maximum(racc[a], jnp.maximum(s[:, 0:128], s[:, 128:256]))
            cacc[b, :, n : n + 256] = jnp.maximum(
                cacc[b, :, n : n + 256], jnp.max(s.reshape(rows // 8, 8, 256), axis=0)
            )

    for b in range(1, slots):
        c_copies[b].wait_recv()
        build(b)

        def with_slot(a, carry, b=b):
            pair(a, b)
            return carry

        lax.fori_loop(0, b, with_slot, 0)

    def rows_to_lanes(x):
        return jnp.max(x.T.reshape(16, 8, 128), axis=0)

    def settle(k, carry):
        for b in range(blocks):
            at = slice(BLK * b, BLK * b + BLK)
            cacc[k, :, at] = jnp.maximum(cacc[k, :, at], rows_to_lanes(racc[k, at, :]))
        return carry

    lax.fori_loop(0, slots, settle, 0)
    b_copies = [None] + [
        remote(cacc.at[k], cret.at[k], b_send.at[k], b_recv.at[k], (g, to_owner[k])) for k in range(1, slots)
    ]

    def listed(which, group, b):
        count = ids_s[which, 4, group]
        hits = jnp.int32(0)
        for j in range(cap):
            hits = hits + ((ids_s[which, group, j] == b) & (j < count)).astype(jnp.int32)
        return hits

    mine = [listed(0, prv, b) for b in range(blocks)]
    theirs = [listed(1, g, b) for b in range(blocks)]
    live = [jnp.where(j < ids_s[1, 4, nxt], 0.0, NEG) for j in range(cap)]

    def tops(x):
        return jnp.max(x.reshape(BLK // 8, 8, BLK), axis=0)

    def own_with(a):
        at = slice(BLK * a, BLK * a + BLK)
        s = dot_nt(own[...], prev[at, :])
        top = f_prev[:, at]
        for b in range(blocks):
            here = slice(BLK * b, BLK * b + BLK)
            x = s[here, :] + jnp.where(mine[a] + theirs[b] > 0, 0.0, NEG)
            f_own[here, :] = jnp.maximum(f_own[here, :], x)
            top = jnp.maximum(top, tops(x))
        f_prev[:, at] = top

    def listed_with(a):
        at = slice(BLK * a, BLK * a + BLK)
        s = dot_nt(lbuf[...], prev[at, :])
        top = f_prev[:, at]
        for j in range(cap):
            here = slice(BLK * j, BLK * j + BLK)
            x = s[here, :] + live[j]
            f_l[here, :] = jnp.maximum(f_l[here, :], x)
            top = jnp.maximum(top, tops(x))
        f_prev[:, at] = top

    for a in range(blocks - 1):
        a_copies[a].wait_recv()
        own_with(a)
    for copy in l_copies:
        copy.wait_recv()
    for a in range(blocks - 1):
        listed_with(a)
    a_copies[blocks - 1].wait_recv()
    listed_with(blocks - 1)
    own_with(blocks - 1)
    for j in range(cap):
        r2s[j] = rows_to_lanes(f_l[BLK * j : BLK * j + BLK, :])
    r_copies = [
        remote(f_prev, r1, r_send.at[0], r_recv.at[0], (prv, m)),
        remote(r2s, r2, r_send.at[1], r_recv.at[1], (nxt, m)),
    ]

    best = cacc[0]
    for k in range(1, slots):
        b_copies[k].wait_recv()
        best = jnp.maximum(best, cret[k])
    coarse[...] = jnp.max(best, axis=0, keepdims=True)

    mine_best = [rows_to_lanes(f_own[BLK * b : BLK * b + BLK, :]) for b in range(blocks)]
    for copy in r_copies:
        copy.wait_recv()
    for b in range(blocks):
        at = slice(BLK * b, BLK * b + BLK)
        x = jnp.maximum(mine_best[b], r1[:, at])
        for j in range(cap):
            x = jnp.maximum(x, r2[j] + jnp.where(ids_s[2, g, j] == b, 0.0, NEG))
        fine[:, at] = jnp.max(x, axis=0, keepdims=True)

    for copy in id_copies + c_copies[1:] + a_copies + l_copies + b_copies[1:] + r_copies:
        copy.wait_send()


def solution(mesh):
    groups, members = mesh.shape["grp"], mesh.shape["mem"]
    cover = COVERS[members]
    slots = len(cover)

    def step(bank, pattern, pair_list, pair_count):
        rows, width = bank.shape
        blocks, group_blocks = pattern.shape
        cap = pair_list.shape[2]
        message = rows // 2 + 48
        bf16, f32, i32 = jnp.bfloat16, jnp.float32, jnp.int32
        vmem = pl.BlockSpec(memory_space=pltpu.VMEM)
        dma = pltpu.SemaphoreType.DMA
        coarse, fine = pl.pallas_call(
            functools.partial(kernel, cover, groups, members),
            out_shape=(jax.ShapeDtypeStruct((1, rows), f32), jax.ShapeDtypeStruct((1, rows), f32)),
            in_specs=[pl.BlockSpec(memory_space=pl.ANY), vmem, vmem, vmem],
            out_specs=(vmem, vmem),
            scratch_shapes=[
                pltpu.VMEM((rows, width), bf16),
                pltpu.VMEM((rows, 128), bf16),
                pltpu.VMEM((rows, width), bf16),
                pltpu.VMEM((cap * BLK, width), bf16),
                pltpu.VMEM((cap * BLK, width), bf16),
                pltpu.VMEM((slots, message, 128), bf16),
                pltpu.VMEM((slots, rows, 128), bf16),
                pltpu.VMEM((slots, rows, 128), bf16),
                pltpu.VMEM((slots, rows, 128), f32),
                pltpu.VMEM((slots, 8, rows), f32),
                pltpu.VMEM((slots, 8, rows), f32),
                pltpu.VMEM((16, 384), i32),
                pltpu.VMEM((384, 128), bf16),
                pltpu.VMEM((3, 8, 128), i32),
                pltpu.SMEM((3, 8, 128), i32),
                pltpu.VMEM((rows, 128), f32),
                pltpu.VMEM((8, rows), f32),
                pltpu.VMEM((cap * BLK, 128), f32),
                pltpu.VMEM((cap, 8, 128), f32),
                pltpu.VMEM((8, rows), f32),
                pltpu.VMEM((cap, 8, 128), f32),
                dma((3,)),
                dma((2,)), dma((2,)),
                dma((slots,)), dma((slots,)),
                dma((blocks,)), dma((blocks,)),
                dma((cap,)), dma((cap,)),
                dma((slots,)), dma((slots,)),
                dma((2,)), dma((2,)),
            ],
            compiler_params=pltpu.CompilerParams(
                collective_id=0, has_side_effects=True, vmem_limit_bytes=40 * 1024 * 1024
            ),
            name="pair_search",
        )(bank, pattern, pair_list, pair_count)
        return coarse.reshape(rows), fine.reshape(rows)

    return jax.shard_map(
        step,
        mesh=mesh,
        in_specs=(
            P(("grp", "mem"), None),
            P(("grp", "mem"), None),
            P(("grp", "mem"), None, None),
            P(("grp", "mem"), None),
        ),
        out_specs=(P(("grp", "mem")), P(("grp", "mem"))),
        check_vma=False,
    )
```

```python
import functools

import jax
import jax.numpy as jnp
from jax import lax
from jax.experimental import pallas as pl
from jax.experimental.pallas import tpu as pltpu
from jax.sharding import PartitionSpec as P

PREF = 64
BLK = 128
NEG = -1e30
MESH = pl.DeviceIdType.MESH
COVERS = {64: (0, 1, 63, 58, 15, 41, 13, 4, 33), 4: (0, 1, 2)}


def dot_nt(a, b):
    return lax.dot_general(a, b, (((1,), (1,)), ((), ())), preferred_element_type=jnp.float32)


def kernel(
    cover, groups, members,
    bank, patt_in, plist_in, pcount_in,
    coarse, fine,
    patt, plist, pcount, own, pre, prev, lbuf, lsend, recv, lhs, rhs, racc, cacc, cret,
    pattpad, sel, ids, ids_s, f_own, f_prev, f_l, r2s, r1, r2,
    loc_sem, id_send, id_recv, c_send, c_recv, a_send, a_recv, l_send, l_recv, b_send, b_recv, r_send, r_recv, go_sem, mem_sem,
):
    g = lax.axis_index("grp")
    m = lax.axis_index("mem")
    core = lax.rem(m, 2)
    nxt = lax.rem(g + 1 + 2 * core, groups)
    prv = lax.rem(g + 3 - 2 * core, groups)
    opp = lax.rem(g + 2, groups)
    slots = len(cover)
    rows = own.shape[0]
    half = rows // 2
    blocks = rows // BLK
    cap = lbuf.shape[0] // BLK
    to_user = [None] + [lax.rem(m + members - d, members) for d in cover[1:]]
    to_owner = [None] + [lax.rem(m + d, members) for d in cover[1:]]

    pre_copy = pltpu.make_async_copy(bank.at[:, pl.ds(0, 128)], pre, loc_sem.at[0])
    pre_copy.start()
    small_copies = [
        pltpu.make_async_copy(src, dst, loc_sem.at[at])
        for src, dst, at in ((plist_in, plist, 3), (pcount_in, pcount, 4), (patt_in, patt, 5))
    ]
    for copy in small_copies:
        copy.start()
    own_copy = pltpu.make_async_copy(bank, own, loc_sem.at[1])
    own_copy.start()

    barrier = pltpu.get_barrier_semaphore()
    for step in range(1, groups):
        other = lax.rem(g + step, groups)

        @pl.when(other != 0)
        def _():
            pl.semaphore_signal(barrier, inc=1, device_id=(other, m), device_id_type=MESH)

    @pl.when(g != 0)
    def _():
        pl.semaphore_wait(barrier, groups - 1)

    @pl.when(g == 1)
    def _():
        pl.semaphore_signal(go_sem, inc=1, device_id=(0, m), device_id_type=MESH)

    @pl.when(g == 0)
    def _():
        pl.semaphore_wait(go_sem, 1)
        for k in range(1, slots):
            for other in (to_user[k], to_owner[k]):
                pl.semaphore_signal(barrier, inc=1, device_id=(0, other), device_id_type=MESH)

    def remote(src, dst, send, rcv, where):
        copy = pltpu.make_async_remote_copy(
            src_ref=src, dst_ref=dst, send_sem=send, recv_sem=rcv, device_id=where, device_id_type=MESH
        )
        copy.start()
        return copy

    ids[0] = jnp.zeros((8, 128), jnp.int32)
    pattpad[...] = jnp.zeros_like(pattpad)
    for copy in small_copies:
        copy.wait()
    ids[0, 0:4, 0:4] = plist[0]
    ids[0, 4:5, 0:4] = pcount[...]
    id_copies = [
        remote(ids.at[0], ids.at[1], id_send.at[0], id_recv.at[0], (nxt, m)),
        remote(ids.at[0], ids.at[2], id_send.at[1], id_recv.at[1], (opp, m)),
    ]
    a_copies = []
    for a in range(blocks):
        part = pl.ds(BLK * a, BLK)
        a_copies.append(remote(bank.at[part, :], prev.at[part, :], a_send.at[a], a_recv.at[a], (nxt, m)))

    lane = lax.broadcasted_iota(jnp.int32, (1, 128), 1)
    low = (lane < PREF).astype(jnp.float32)

    for t in range(3):
        pattpad[8 * t : 8 * t + blocks, :] = patt[:, 128 * t : 128 * t + 128]
    recv[0, half : half + 32, :] = pattpad[...].astype(jnp.float32).astype(jnp.bfloat16)
    pre_copy.wait()
    recv[0, 0:half, :] = (
        pre[0:half, :].astype(jnp.float32) * low
        + pltpu.roll(pre[half:rows, :].astype(jnp.float32) * low, PREF, 1)
    ).astype(jnp.bfloat16)

    own_copy.wait()
    for copy in id_copies:
        copy.wait_recv()
    id_local = pltpu.make_async_copy(ids, ids_s, loc_sem.at[2])
    id_local.start()
    id_local.wait()
    l_copies = []
    for j in range(cap):
        block = ids_s[2, g, j]
        picked = own[0:BLK, :]
        for b in range(1, blocks):
            picked = lax.select(block == b, own[BLK * b : BLK * b + BLK, :], picked)
        lsend[BLK * j : BLK * j + BLK, :] = picked
        part = pl.ds(BLK * j, BLK)
        l_copies.append(remote(lsend.at[part, :], lbuf.at[part, :], l_send.at[j], l_recv.at[j], (prv, m)))

    @pl.when(g == 0)
    def _():
        pl.semaphore_wait(barrier, 2 * (slots - 1))
        for other in range(1, groups):
            pl.semaphore_signal(mem_sem, inc=1, device_id=(other, m), device_id_type=MESH)

    @pl.when(g != 0)
    def _():
        pl.semaphore_wait(mem_sem, 1)

    c_copies = [None] + [
        remote(recv.at[0], recv.at[k], c_send.at[k], c_recv.at[k], (g, to_user[k])) for k in range(1, slots)
    ]

    column = jnp.full((1, 128), -1, jnp.int32)
    for k in range(slots):
        first = PREF + blocks * k
        member = m if k == 0 else to_owner[k]
        column = jnp.where((lane >= first) & (lane < first + blocks), blocks * member + lane - first, column)
    row_id = lax.broadcasted_iota(jnp.int32, sel.shape, 0)
    sel[...] = (row_id == column).astype(jnp.float32).astype(jnp.bfloat16)
    in_mask = ((lane >= PREF) & (lane < PREF + blocks * slots)).astype(jnp.float32)

    def build(k):
        parts = [
            jnp.dot(
                recv[k, half + 16 * (t // 2) : half + 16 * (t // 2) + 16, :],
                sel[128 * t : 128 * t + 128, :],
                preferred_element_type=jnp.float32,
            )
            for t in range(3)
        ]
        bias = parts[0][0:8] + parts[1][8:16] + parts[2][0:8]
        bias = (bias - 1.0) * (-NEG) * in_mask
        for b in range(blocks):
            at = BLK * (b % (blocks // 2))
            part = recv[k, at : at + BLK, :].astype(jnp.float32)
            if b >= blocks // 2:
                part = pltpu.roll(part, PREF, 1)
            part = part * low
            hot = (lane == PREF + blocks * k + b).astype(jnp.float32)
            lhs[k, BLK * b : BLK * b + BLK, :] = (part + hot).astype(jnp.bfloat16)
            rhs[k, BLK * b : BLK * b + BLK, :] = (part + bias[b : b + 1, :]).astype(jnp.bfloat16)

    f_own[...] = jnp.full_like(f_own, NEG)
    f_prev[...] = jnp.full_like(f_prev, NEG)
    f_l[...] = jnp.full_like(f_l, NEG)

    def tops(x):
        return jnp.max(x.reshape(BLK // 8, 8, BLK), axis=0)

    def rows_to_lanes(x):
        return jnp.max(x.T.reshape(16, 8, 128), axis=0)

    build(0)
    diag = jnp.where(
        lax.broadcasted_iota(jnp.int32, (BLK, BLK), 0) == lax.broadcasted_iota(jnp.int32, (BLK, BLK), 1), NEG, 0.0
    )
    for c in range(blocks):
        part = slice(BLK * c, BLK * c + BLK)
        s = dot_nt(lhs[0], rhs[0, part, :])
        top = jnp.full((8, BLK), NEG, jnp.float32)
        for b in range(blocks):
            x = s[BLK * b : BLK * b + BLK, :]
            if b == c:
                x = x + diag
            top = jnp.maximum(top, tops(x))
        cacc[0, :, part] = top

    done = set()

    def shard(b):
        c_copies[b].wait_recv()
        build(b)
        racc[...] = jnp.full_like(racc, NEG)
        for a in range(b):
            gap = (cover[a] - cover[b]) % members
            if min(gap, members - gap) in done:
                continue
            done.add(min(gap, members - gap))
            for n in range(0, rows, 256):
                s = dot_nt(lhs[b], rhs[a, n : n + 256, :])
                racc[...] = jnp.maximum(racc[...], jnp.maximum(s[:, 0:128], s[:, 128:256]))
                cacc[a, :, n : n + 256] = jnp.maximum(
                    cacc[a, :, n : n + 256], jnp.max(s.reshape(rows // 8, 8, 256), axis=0)
                )
        for c in range(blocks):
            at = slice(BLK * c, BLK * c + BLK)
            cacc[b, :, at] = rows_to_lanes(racc[at, :])

    def listed(which, group, b):
        count = ids_s[which, 4, group]
        hits = jnp.int32(0)
        for j in range(cap):
            hits = hits + ((ids_s[which, group, j] == b) & (j < count)).astype(jnp.int32)
        return hits

    mine = [listed(0, prv, b) for b in range(blocks)]
    theirs = [listed(1, g, b) for b in range(blocks)]
    live = [jnp.where(j < ids_s[1, 4, nxt], 0.0, NEG) for j in range(cap)]

    def own_with(first, last):
        for a in range(first, last):
            a_copies[a].wait_recv()
        s = dot_nt(own[...], prev[BLK * first : BLK * last, :])
        for a in range(first, last):
            at = slice(BLK * a, BLK * a + BLK)
            top = f_prev[:, at]
            for b in range(blocks):
                here = slice(BLK * b, BLK * b + BLK)
                x = s[here, BLK * (a - first) : BLK * (a - first) + BLK]
                x = x + jnp.where(mine[a] + theirs[b] > 0, 0.0, NEG)
                f_own[here, :] = jnp.maximum(f_own[here, :], x)
                top = jnp.maximum(top, tops(x))
            f_prev[:, at] = top

    def listed_with(first, last):
        s = dot_nt(lbuf[...], prev[BLK * first : BLK * last, :])
        for a in range(first, last):
            at = slice(BLK * a, BLK * a + BLK)
            top = f_prev[:, at]
            for j in range(cap):
                here = slice(BLK * j, BLK * j + BLK)
                x = s[here, BLK * (a - first) : BLK * (a - first) + BLK] + live[j]
                f_l[here, :] = jnp.maximum(f_l[here, :], x)
                top = jnp.maximum(top, tops(x))
            f_prev[:, at] = top

    early = {slots // 2: (0, 1), 3 * slots // 4: (1, 2)}
    for b in range(1, slots):
        shard(b)
        if b in early:
            own_with(*early[b])
    b_copies = [None] + [
        remote(cacc.at[k], cret.at[k], b_send.at[k], b_recv.at[k], (g, to_owner[k])) for k in range(1, slots)
    ]
    own_with(2, 4)
    for copy in l_copies:
        copy.wait_recv()
    listed_with(0, 4)
    own_with(4, 5)
    listed_with(4, 5)
    own_with(5, 6)
    listed_with(5, 6)
    for j in range(cap):
        r2s[j] = rows_to_lanes(f_l[BLK * j : BLK * j + BLK, :])
    r_copies = [
        remote(f_prev, r1, r_send.at[0], r_recv.at[0], (prv, m)),
        remote(r2s, r2, r_send.at[1], r_recv.at[1], (nxt, m)),
    ]

    best = cacc[0]
    for k in range(1, slots):
        b_copies[k].wait_recv()
        best = jnp.maximum(best, cret[k])
    coarse[...] = jnp.max(best, axis=0)

    mine_best = [rows_to_lanes(f_own[BLK * b : BLK * b + BLK, :]) for b in range(blocks)]
    for copy in r_copies:
        copy.wait_recv()
    for b in range(blocks):
        at = slice(BLK * b, BLK * b + BLK)
        x = jnp.maximum(mine_best[b], r1[:, at])
        for j in range(cap):
            x = jnp.maximum(x, r2[j] + jnp.where(ids_s[2, g, j] == b, 0.0, NEG))
        fine[at] = jnp.max(x, axis=0)

    for copy in id_copies + c_copies[1:] + a_copies + l_copies + b_copies[1:] + r_copies:
        copy.wait_send()


def solution(mesh):
    groups, members = mesh.shape["grp"], mesh.shape["mem"]
    cover = COVERS[members]
    slots = len(cover)

    def step(bank, pattern, pair_list, pair_count):
        rows, width = bank.shape
        blocks, group_blocks = pattern.shape
        cap = pair_list.shape[2]
        message = rows // 2 + 32
        bf16, f32, i32 = jnp.bfloat16, jnp.float32, jnp.int32
        vmem = pl.BlockSpec(memory_space=pltpu.VMEM)
        dma = pltpu.SemaphoreType.DMA
        coarse, fine = pl.pallas_call(
            functools.partial(kernel, cover, groups, members),
            out_shape=(jax.ShapeDtypeStruct((rows,), f32), jax.ShapeDtypeStruct((rows,), f32)),
            in_specs=[pl.BlockSpec(memory_space=pltpu.HBM)] * 4,
            out_specs=(vmem, vmem),
            scratch_shapes=[
                pltpu.VMEM(pattern.shape, i32),
                pltpu.VMEM(pair_list.shape, i32),
                pltpu.VMEM(pair_count.shape, i32),
                pltpu.VMEM((rows, width), bf16),
                pltpu.VMEM((rows, 128), bf16),
                pltpu.VMEM((rows, width), bf16),
                pltpu.VMEM((cap * BLK, width), bf16),
                pltpu.VMEM((cap * BLK, width), bf16),
                pltpu.VMEM((slots, message, 128), bf16),
                pltpu.VMEM((slots, rows, 128), bf16),
                pltpu.VMEM((slots, rows, 128), bf16),
                pltpu.VMEM((rows, 128), f32),
                pltpu.VMEM((slots, 8, rows), f32),
                pltpu.VMEM((slots, 8, rows), f32),
                pltpu.VMEM((32, 128), i32),
                pltpu.VMEM((384, 128), bf16),
                pltpu.VMEM((3, 8, 128), i32),
                pltpu.SMEM((3, 8, 128), i32),
                pltpu.VMEM((rows, 128), f32),
                pltpu.VMEM((8, rows), f32),
                pltpu.VMEM((cap * BLK, 128), f32),
                pltpu.VMEM((cap, 8, 128), f32),
                pltpu.VMEM((8, rows), f32),
                pltpu.VMEM((cap, 8, 128), f32),
                dma((6,)),
                dma((2,)), dma((2,)),
                dma((slots,)), dma((slots,)),
                dma((blocks,)), dma((blocks,)),
                dma((cap,)), dma((cap,)),
                dma((slots,)), dma((slots,)),
                dma((2,)), dma((2,)),
                pltpu.SemaphoreType.REGULAR,
                pltpu.SemaphoreType.REGULAR,
            ],
            compiler_params=pltpu.CompilerParams(
                collective_id=0, has_side_effects=True, vmem_limit_bytes=60 * 1024 * 1024
            ),
            name="pair_search",
        )(bank, pattern, pair_list, pair_count)
        return coarse, fine

    return jax.shard_map(
        step,
        mesh=mesh,
        in_specs=(
            P(("grp", "mem"), None),
            P(("grp", "mem"), None),
            P(("grp", "mem"), None, None),
            P(("grp", "mem"), None),
        ),
        out_specs=(P(("grp", "mem")), P(("grp", "mem"))),
        check_vma=False,
    )
```

```python
import functools

import jax
import jax.numpy as jnp
from jax import lax
from jax.experimental import pallas as pl
from jax.experimental.pallas import tpu as pltpu
from jax.sharding import PartitionSpec as P

PREF = 64
BLK = 128
NEG = -1e30
MESH = pl.DeviceIdType.MESH
COVERS = {64: (0, 1, 2, 16, 5, 34, 14, 59, 42), 4: (0, 1, 2)}


def dot_nt(a, b):
    return lax.dot_general(a, b, (((1,), (1,)), ((), ())), preferred_element_type=jnp.float32)


def shifted(m, d, members):
    if members != 64:
        return lax.rem(m + d, members)
    at = lax.rem(((m // 2) % 4) * 16 + (m // 8) * 2 + m % 2 + d, members)
    return ((at // 2) % 8) * 8 + (at // 16) * 2 + at % 2


def kernel(
    cover, groups, members,
    bank, patt_in, plist_in, pcount_in,
    out,
    patt, plist, pcount, own, pre, prev, lbuf, lsend, recv, lhs, rhs, racc, cacc, cret,
    pattpad, sel, ids, ids_s, f_own, f_prev, f_l, r2s, r1, r2,
    loc_sem, id_send, id_recv, c_send, c_recv, a_send, a_recv, l_send, l_recv, b_send, b_recv, r_send, r_recv, go_sem, mem_sem,
):
    g = lax.axis_index("grp")
    m = lax.axis_index("mem")
    core = lax.rem(m, 2)
    nxt = lax.rem(g + 1 + 2 * core, groups)
    prv = lax.rem(g + 3 - 2 * core, groups)
    opp = lax.rem(g + 2, groups)
    slots = len(cover)
    rows = own.shape[0]
    half = rows // 2
    blocks = rows // BLK
    cap = lbuf.shape[0] // BLK
    to_user = [None] + [shifted(m, members - d, members) for d in cover[1:]]
    to_owner = [None] + [shifted(m, d, members) for d in cover[1:]]

    pre_copy = pltpu.make_async_copy(bank.at[:, pl.ds(0, 128)], pre, loc_sem.at[0])
    pre_copy.start()
    small_copies = [
        pltpu.make_async_copy(src, dst, loc_sem.at[at])
        for src, dst, at in ((plist_in, plist, 3), (pcount_in, pcount, 4), (patt_in, patt, 5))
    ]
    for copy in small_copies:
        copy.start()
    own_copy = pltpu.make_async_copy(bank, own, loc_sem.at[1])
    own_copy.start()

    barrier = pltpu.get_barrier_semaphore()
    for step in range(1, groups):
        other = lax.rem(g + step, groups)

        @pl.when(other != 0)
        def _():
            pl.semaphore_signal(barrier, inc=1, device_id=(other, m), device_id_type=MESH)

    @pl.when(g != 0)
    def _():
        pl.semaphore_wait(barrier, groups - 1)

    @pl.when(g == 1)
    def _():
        pl.semaphore_signal(go_sem, inc=1, device_id=(0, m), device_id_type=MESH)

    @pl.when(g == 1)
    def _():
        for k in range(1, slots):
            for other in (to_user[k], to_owner[k]):
                pl.semaphore_signal(barrier, inc=1, device_id=(0, other), device_id_type=MESH)

    @pl.when(g == 0)
    def _():
        pl.semaphore_wait(go_sem, 1)

    def planned(src, dst, send, rcv, where):
        return pltpu.make_async_remote_copy(
            src_ref=src, dst_ref=dst, send_sem=send, recv_sem=rcv, device_id=where, device_id_type=MESH
        )

    def remote(*args):
        copy = planned(*args)
        copy.start()
        return copy

    ids[0] = jnp.zeros((8, 128), jnp.int32)
    pattpad[...] = jnp.zeros_like(pattpad)
    for copy in small_copies:
        copy.wait()
    ids[0, 0:4, 0:4] = plist[0]
    ids[0, 4:5, 0:4] = pcount[...]
    id_copies = [
        remote(ids.at[0], ids.at[1], id_send.at[0], id_recv.at[0], (nxt, m)),
        remote(ids.at[0], ids.at[2], id_send.at[1], id_recv.at[1], (opp, m)),
    ]
    a_copies = []
    for a in range(blocks):
        part = pl.ds(BLK * a, BLK)
        a_copies.append(remote(bank.at[part, :], prev.at[part, :], a_send.at[a], a_recv.at[a], (nxt, m)))

    lane = lax.broadcasted_iota(jnp.int32, (1, 128), 1)
    low = (lane < PREF).astype(jnp.float32)

    for t in range(3):
        pattpad[8 * t : 8 * t + blocks, :] = patt[:, 128 * t : 128 * t + 128]
    recv[0, half : half + 32, :] = pattpad[...].astype(jnp.float32).astype(jnp.bfloat16)
    pre_copy.wait()
    recv[0, 0:half, :] = (
        pre[0:half, :].astype(jnp.float32) * low
        + pltpu.roll(pre[half:rows, :].astype(jnp.float32) * low, PREF, 1)
    ).astype(jnp.bfloat16)

    c_copies = [None] + [
        planned(recv.at[0], recv.at[k], c_send.at[k], c_recv.at[k], (g, to_user[k])) for k in range(1, slots)
    ]

    def send_prefixes():
        @pl.when(g == 0)
        def _():
            pl.semaphore_wait(barrier, 2 * (slots - 1))
            for other in range(1, groups):
                pl.semaphore_signal(mem_sem, inc=1, device_id=(other, m), device_id_type=MESH)

        @pl.when(g != 0)
        def _():
            pl.semaphore_wait(mem_sem, 1)

        for copy in c_copies[1:]:
            copy.start()

    late = m // (members // 2)
    pl.when(late == 1)(send_prefixes)

    own_copy.wait()
    for copy in id_copies:
        copy.wait_recv()
    id_local = pltpu.make_async_copy(ids, ids_s, loc_sem.at[2])
    id_local.start()
    id_local.wait()
    l_copies = []
    for j in range(cap):
        block = ids_s[2, g, j]
        picked = own[0:BLK, :]
        for b in range(1, blocks):
            picked = lax.select(block == b, own[BLK * b : BLK * b + BLK, :], picked)
        lsend[BLK * j : BLK * j + BLK, :] = picked
        part = pl.ds(BLK * j, BLK)
        l_copies.append(remote(lsend.at[part, :], lbuf.at[part, :], l_send.at[j], l_recv.at[j], (prv, m)))

    pl.when(late == 0)(send_prefixes)

    column = jnp.full((1, 128), -1, jnp.int32)
    for k in range(slots):
        first = PREF + blocks * k
        member = m if k == 0 else to_owner[k]
        column = jnp.where((lane >= first) & (lane < first + blocks), blocks * member + lane - first, column)
    row_id = lax.broadcasted_iota(jnp.int32, sel.shape, 0)
    sel[...] = (row_id == column).astype(jnp.float32).astype(jnp.bfloat16)
    in_mask = ((lane >= PREF) & (lane < PREF + blocks * slots)).astype(jnp.float32)

    def build(k):
        parts = [
            jnp.dot(
                recv[k, half + 16 * (t // 2) : half + 16 * (t // 2) + 16, :],
                sel[128 * t : 128 * t + 128, :],
                preferred_element_type=jnp.float32,
            )
            for t in range(3)
        ]
        bias = parts[0][0:8] + parts[1][8:16] + parts[2][0:8]
        bias = (bias - 1.0) * (-NEG) * in_mask
        for b in range(blocks):
            at = BLK * (b % (blocks // 2))
            part = recv[k, at : at + BLK, :].astype(jnp.float32)
            if b >= blocks // 2:
                part = pltpu.roll(part, PREF, 1)
            part = part * low
            hot = (lane == PREF + blocks * k + b).astype(jnp.float32)
            lhs[k, BLK * b : BLK * b + BLK, :] = (part + hot).astype(jnp.bfloat16)
            rhs[k, BLK * b : BLK * b + BLK, :] = (part + bias[b : b + 1, :]).astype(jnp.bfloat16)

    f_own[...] = jnp.full_like(f_own, NEG)
    f_prev[...] = jnp.full_like(f_prev, NEG)
    f_l[...] = jnp.full_like(f_l, NEG)

    def tops(x):
        return jnp.max(x.reshape(BLK // 8, 8, BLK), axis=0)

    def rows_to_lanes(x):
        return jnp.max(x.T.reshape(16, 8, 128), axis=0)

    build(0)
    diag = jnp.where(
        lax.broadcasted_iota(jnp.int32, (BLK, BLK), 0) == lax.broadcasted_iota(jnp.int32, (BLK, BLK), 1), NEG, 0.0
    )
    for c in range(blocks):
        part = slice(BLK * c, BLK * c + BLK)
        s = dot_nt(lhs[0], rhs[0, part, :])
        top = jnp.full((8, BLK), NEG, jnp.float32)
        for b in range(blocks):
            x = s[BLK * b : BLK * b + BLK, :]
            if b == c:
                x = x + diag
            top = jnp.maximum(top, tops(x))
        cacc[0, :, part] = top

    done = set()

    def shard(b):
        c_copies[b].wait_recv()
        build(b)
        racc[...] = jnp.full_like(racc, NEG)
        for a in range(b):
            gap = (cover[a] - cover[b]) % members
            if min(gap, members - gap) in done:
                continue
            done.add(min(gap, members - gap))
            for n in range(0, rows, 256):
                s = dot_nt(lhs[b], rhs[a, n : n + 256, :])
                racc[...] = jnp.maximum(racc[...], jnp.maximum(s[:, 0:128], s[:, 128:256]))
                cacc[a, :, n : n + 256] = jnp.maximum(
                    cacc[a, :, n : n + 256], jnp.max(s.reshape(rows // 8, 8, 256), axis=0)
                )
        for c in range(blocks):
            at = slice(BLK * c, BLK * c + BLK)
            cacc[b, :, at] = rows_to_lanes(racc[at, :])

    def listed(which, group, b):
        count = ids_s[which, 4, group]
        hits = jnp.int32(0)
        for j in range(cap):
            hits = hits + ((ids_s[which, group, j] == b) & (j < count)).astype(jnp.int32)
        return hits

    mine = [listed(0, prv, b) for b in range(blocks)]
    theirs = [listed(1, g, b) for b in range(blocks)]
    live = [jnp.where(j < ids_s[1, 4, nxt], 0.0, NEG) for j in range(cap)]

    def own_with(first, last):
        for a in range(first, last):
            a_copies[a].wait_recv()
        s = dot_nt(own[...], prev[BLK * first : BLK * last, :])
        for a in range(first, last):
            at = slice(BLK * a, BLK * a + BLK)
            top = f_prev[:, at]
            for b in range(blocks):
                here = slice(BLK * b, BLK * b + BLK)
                x = s[here, BLK * (a - first) : BLK * (a - first) + BLK]
                x = x + jnp.where(mine[a] + theirs[b] > 0, 0.0, NEG)
                f_own[here, :] = jnp.maximum(f_own[here, :], x)
                top = jnp.maximum(top, tops(x))
            f_prev[:, at] = top

    def listed_with(first, last):
        s = dot_nt(lbuf[...], prev[BLK * first : BLK * last, :])
        for a in range(first, last):
            at = slice(BLK * a, BLK * a + BLK)
            top = f_prev[:, at]
            for j in range(cap):
                here = slice(BLK * j, BLK * j + BLK)
                x = s[here, BLK * (a - first) : BLK * (a - first) + BLK] + live[j]
                f_l[here, :] = jnp.maximum(f_l[here, :], x)
                top = jnp.maximum(top, tops(x))
            f_prev[:, at] = top

    for b in range(1, slots):
        shard(b)
    b_copies = [None] + [
        remote(cacc.at[k], cret.at[k], b_send.at[k], b_recv.at[k], (g, to_owner[k])) for k in range(1, slots)
    ]
    own_with(0, blocks)
    for copy in l_copies:
        copy.wait_recv()
    listed_with(0, blocks)
    for j in range(cap):
        r2s[j] = rows_to_lanes(f_l[BLK * j : BLK * j + BLK, :])
    r_copies = [
        remote(f_prev, r1, r_send.at[0], r_recv.at[0], (prv, m)),
        remote(r2s, r2, r_send.at[1], r_recv.at[1], (nxt, m)),
    ]

    best = cacc[0]
    for k in range(1, slots):
        b_copies[k].wait_recv()
        best = jnp.maximum(best, cret[k])
    out[0:1, :] = jnp.max(best, axis=0, keepdims=True)

    mine_best = [rows_to_lanes(f_own[BLK * b : BLK * b + BLK, :]) for b in range(blocks)]
    for copy in r_copies:
        copy.wait_recv()
    for b in range(blocks):
        at = slice(BLK * b, BLK * b + BLK)
        x = jnp.maximum(mine_best[b], r1[:, at])
        for j in range(cap):
            x = jnp.maximum(x, r2[j] + jnp.where(ids_s[2, g, j] == b, 0.0, NEG))
        out[1:2, at] = jnp.max(x, axis=0, keepdims=True)

    for copy in id_copies + c_copies[1:] + a_copies + l_copies + b_copies[1:] + r_copies:
        copy.wait_send()


def solution(mesh):
    groups, members = mesh.shape["grp"], mesh.shape["mem"]
    cover = COVERS[members]
    slots = len(cover)

    def step(bank, pattern, pair_list, pair_count):
        rows, width = bank.shape
        blocks, group_blocks = pattern.shape
        cap = pair_list.shape[2]
        message = rows // 2 + 32
        bf16, f32, i32 = jnp.bfloat16, jnp.float32, jnp.int32
        vmem = pl.BlockSpec(memory_space=pltpu.VMEM)
        dma = pltpu.SemaphoreType.DMA
        out = pl.pallas_call(
            functools.partial(kernel, cover, groups, members),
            out_shape=jax.ShapeDtypeStruct((2, rows), f32),
            in_specs=[pl.BlockSpec(memory_space=pltpu.HBM)] * 4,
            out_specs=vmem,
            scratch_shapes=[
                pltpu.VMEM(pattern.shape, i32),
                pltpu.VMEM(pair_list.shape, i32),
                pltpu.VMEM(pair_count.shape, i32),
                pltpu.VMEM((rows, width), bf16),
                pltpu.VMEM((rows, 128), bf16),
                pltpu.VMEM((rows, width), bf16),
                pltpu.VMEM((cap * BLK, width), bf16),
                pltpu.VMEM((cap * BLK, width), bf16),
                pltpu.VMEM((slots, message, 128), bf16),
                pltpu.VMEM((slots, rows, 128), bf16),
                pltpu.VMEM((slots, rows, 128), bf16),
                pltpu.VMEM((rows, 128), f32),
                pltpu.VMEM((slots, 8, rows), f32),
                pltpu.VMEM((slots, 8, rows), f32),
                pltpu.VMEM((32, 128), i32),
                pltpu.VMEM((384, 128), bf16),
                pltpu.VMEM((3, 8, 128), i32),
                pltpu.SMEM((3, 8, 128), i32),
                pltpu.VMEM((rows, 128), f32),
                pltpu.VMEM((8, rows), f32),
                pltpu.VMEM((cap * BLK, 128), f32),
                pltpu.VMEM((cap, 8, 128), f32),
                pltpu.VMEM((8, rows), f32),
                pltpu.VMEM((cap, 8, 128), f32),
                dma((6,)),
                dma((2,)), dma((2,)),
                dma((slots,)), dma((slots,)),
                dma((blocks,)), dma((blocks,)),
                dma((cap,)), dma((cap,)),
                dma((slots,)), dma((slots,)),
                dma((2,)), dma((2,)),
                pltpu.SemaphoreType.REGULAR,
                pltpu.SemaphoreType.REGULAR,
            ],
            compiler_params=pltpu.CompilerParams(
                collective_id=0, has_side_effects=True, vmem_limit_bytes=60 * 1024 * 1024
            ),
            name="pair_search",
        )(bank, pattern, pair_list, pair_count)
        return out[0], out[1]

    return jax.shard_map(
        step,
        mesh=mesh,
        in_specs=(
            P(("grp", "mem"), None),
            P(("grp", "mem"), None),
            P(("grp", "mem"), None, None),
            P(("grp", "mem"), None),
        ),
        out_specs=(P(("grp", "mem")), P(("grp", "mem"))),
        check_vma=False,
    )
```

```python
import functools

import jax
import jax.numpy as jnp
from jax import lax
from jax.experimental import pallas as pl
from jax.experimental.pallas import tpu as pltpu
from jax.sharding import PartitionSpec as P

PREF = 64
BLK = 128
NEG = -1e30
MESH = pl.DeviceIdType.MESH
COVERS = {64: (0, 1, 2, 16, 5, 34, 14, 59, 42), 4: (0, 1, 2)}


def dot_nt(a, b):
    return lax.dot_general(a, b, (((1,), (1,)), ((), ())), preferred_element_type=jnp.float32)


def shifted(m, d, members):
    if members != 64:
        return lax.rem(m + d, members)
    at = lax.rem(((m // 2) % 4) * 16 + (m // 8) * 2 + m % 2 + d, members)
    return ((at // 2) % 8) * 8 + (at // 16) * 2 + at % 2


def kernel(
    cover, groups, members,
    bank, patt_in, plist_in, pcount_in,
    out,
    patt, plist, pcount, own, pre, prev, lbuf, lsend, recv, lhs, rhs, racc, cacc, crow, cret,
    pattpad, sel, ids, ids_s, f_own, f_prev, f_row, f_l, r2s, r1, r2,
    loc_sem, id_send, id_recv, c_send, c_recv, a_send, a_recv, l_send, l_recv, b_send, b_recv, r_send, r_recv, go_sem, mem_sem,
):
    g = lax.axis_index("grp")
    m = lax.axis_index("mem")
    core = lax.rem(m, 2)
    nxt = lax.rem(g + 1 + 2 * core, groups)
    prv = lax.rem(g + 3 - 2 * core, groups)
    opp = lax.rem(g + 2, groups)
    slots = len(cover)
    rows = own.shape[0]
    half = rows // 2
    blocks = rows // BLK
    cap = lbuf.shape[0] // BLK
    to_user = [None] + [shifted(m, members - d, members) for d in cover[1:]]
    to_owner = [None] + [shifted(m, d, members) for d in cover[1:]]

    pre_copy = pltpu.make_async_copy(bank.at[:, pl.ds(0, 128)], pre, loc_sem.at[0])
    pre_copy.start()
    small_copies = [
        pltpu.make_async_copy(src, dst, loc_sem.at[at])
        for src, dst, at in ((plist_in, plist, 3), (pcount_in, pcount, 4), (patt_in, patt, 5))
    ]
    for copy in small_copies:
        copy.start()
    own_copy = pltpu.make_async_copy(bank, own, loc_sem.at[1])
    own_copy.start()

    barrier = pltpu.get_barrier_semaphore()
    for step in range(1, groups):
        other = lax.rem(g + step, groups)

        @pl.when(other != 0)
        def _():
            pl.semaphore_signal(barrier, inc=1, device_id=(other, m), device_id_type=MESH)

    @pl.when(g != 0)
    def _():
        pl.semaphore_wait(barrier, groups - 1)

    @pl.when(g == 1)
    def _():
        pl.semaphore_signal(go_sem, inc=1, device_id=(0, m), device_id_type=MESH)

    @pl.when(g == 1)
    def _():
        for k in range(1, slots):
            for other in (to_user[k], to_owner[k]):
                pl.semaphore_signal(barrier, inc=1, device_id=(0, other), device_id_type=MESH)

    @pl.when(g == 0)
    def _():
        pl.semaphore_wait(go_sem, 1)

    def planned(src, dst, send, rcv, where):
        return pltpu.make_async_remote_copy(
            src_ref=src, dst_ref=dst, send_sem=send, recv_sem=rcv, device_id=where, device_id_type=MESH
        )

    def remote(*args):
        copy = planned(*args)
        copy.start()
        return copy

    ids[0] = jnp.zeros((8, 128), jnp.int32)
    pattpad[...] = jnp.zeros_like(pattpad)
    for copy in small_copies:
        copy.wait()
    ids[0, 0:4, 0:4] = plist[0]
    ids[0, 4:5, 0:4] = pcount[...]
    id_copies = [
        remote(ids.at[0], ids.at[1], id_send.at[0], id_recv.at[0], (nxt, m)),
        remote(ids.at[0], ids.at[2], id_send.at[1], id_recv.at[1], (opp, m)),
    ]
    a_copies = []
    for a in range(blocks):
        part = pl.ds(BLK * a, BLK)
        a_copies.append(remote(bank.at[part, :], prev.at[part, :], a_send.at[a], a_recv.at[a], (nxt, m)))

    lane = lax.broadcasted_iota(jnp.int32, (1, 128), 1)
    low = (lane < PREF).astype(jnp.float32)

    for t in range(3):
        pattpad[8 * t : 8 * t + blocks, :] = patt[:, 128 * t : 128 * t + 128]
    recv[0, half : half + 32, :] = pattpad[...].astype(jnp.float32).astype(jnp.bfloat16)
    pre_copy.wait()
    recv[0, 0:half, :] = (
        pre[0:half, :].astype(jnp.float32) * low
        + pltpu.roll(pre[half:rows, :].astype(jnp.float32) * low, PREF, 1)
    ).astype(jnp.bfloat16)

    c_copies = [None] + [
        planned(recv.at[0], recv.at[k], c_send.at[k], c_recv.at[k], (g, to_user[k])) for k in range(1, slots)
    ]

    def send_prefixes():
        @pl.when(g == 0)
        def _():
            pl.semaphore_wait(barrier, 2 * (slots - 1))
            for other in range(1, groups):
                pl.semaphore_signal(mem_sem, inc=1, device_id=(other, m), device_id_type=MESH)

        @pl.when(g != 0)
        def _():
            pl.semaphore_wait(mem_sem, 1)

        for copy in c_copies[1:]:
            copy.start()

    late = m // (members // 2)
    pl.when(late == 1)(send_prefixes)

    own_copy.wait()
    for copy in id_copies:
        copy.wait_recv()
    id_local = pltpu.make_async_copy(ids, ids_s, loc_sem.at[2])
    id_local.start()
    id_local.wait()
    l_copies = []
    for j in range(cap):
        block = ids_s[2, g, j]
        picked = own[0:BLK, :]
        for b in range(1, blocks):
            picked = lax.select(block == b, own[BLK * b : BLK * b + BLK, :], picked)
        lsend[BLK * j : BLK * j + BLK, :] = picked
        part = pl.ds(BLK * j, BLK)
        l_copies.append(remote(lsend.at[part, :], lbuf.at[part, :], l_send.at[j], l_recv.at[j], (prv, m)))

    pl.when(late == 0)(send_prefixes)

    column = jnp.full((1, 128), -1, jnp.int32)
    for k in range(slots):
        first = PREF + blocks * k
        member = m if k == 0 else to_owner[k]
        column = jnp.where((lane >= first) & (lane < first + blocks), blocks * member + lane - first, column)
    row_id = lax.broadcasted_iota(jnp.int32, sel.shape, 0)
    sel[...] = (row_id == column).astype(jnp.float32).astype(jnp.bfloat16)
    in_mask = ((lane >= PREF) & (lane < PREF + blocks * slots)).astype(jnp.float32)

    def build(k):
        parts = [
            jnp.dot(
                recv[k, half + 16 * (t // 2) : half + 16 * (t // 2) + 16, :],
                sel[128 * t : 128 * t + 128, :],
                preferred_element_type=jnp.float32,
            )
            for t in range(3)
        ]
        bias = parts[0][0:8] + parts[1][8:16] + parts[2][0:8]
        bias = (bias - 1.0) * (-NEG) * in_mask
        for b in range(blocks):
            at = BLK * (b % (blocks // 2))
            part = recv[k, at : at + BLK, :].astype(jnp.float32)
            if b >= blocks // 2:
                part = pltpu.roll(part, PREF, 1)
            part = part * low
            hot = (lane == PREF + blocks * k + b).astype(jnp.float32)
            lhs[k, BLK * b : BLK * b + BLK, :] = (part + hot).astype(jnp.bfloat16)
            rhs[k, BLK * b : BLK * b + BLK, :] = (part + bias[b : b + 1, :]).astype(jnp.bfloat16)

    f_own[...] = jnp.full_like(f_own, NEG)
    f_prev[...] = jnp.full_like(f_prev, NEG)
    f_l[...] = jnp.full_like(f_l, NEG)

    def tops(x):
        return jnp.max(x.reshape(BLK // 8, 8, BLK), axis=0)

    def rows_to_lanes(x):
        return jnp.max(x.T.reshape(16, 8, 128), axis=0)

    build(0)
    diag = jnp.where(
        lax.broadcasted_iota(jnp.int32, (BLK, BLK), 0) == lax.broadcasted_iota(jnp.int32, (BLK, BLK), 1), NEG, 0.0
    )
    for c in range(blocks):
        part = slice(BLK * c, BLK * c + BLK)
        s = dot_nt(lhs[0], rhs[0, part, :])
        top = jnp.full((8, BLK), NEG, jnp.float32)
        for b in range(blocks):
            x = s[BLK * b : BLK * b + BLK, :]
            if b == c:
                x = x + diag
            top = jnp.maximum(top, tops(x))
        cacc[0, :, part] = top

    done = set()

    def shard(b):
        c_copies[b].wait_recv()
        build(b)
        racc[...] = jnp.full_like(racc, NEG)
        for a in range(b):
            gap = (cover[a] - cover[b]) % members
            if min(gap, members - gap) in done:
                continue
            done.add(min(gap, members - gap))
            for n in range(0, rows, 256):
                s = dot_nt(lhs[b], rhs[a, n : n + 256, :])
                racc[...] = jnp.maximum(racc[...], jnp.maximum(s[:, 0:128], s[:, 128:256]))
                cacc[a, :, n : n + 256] = jnp.maximum(
                    cacc[a, :, n : n + 256], jnp.max(s.reshape(rows // 8, 8, 256), axis=0)
                )
        for c in range(blocks):
            at = slice(BLK * c, BLK * c + BLK)
            cacc[b, :, at] = rows_to_lanes(racc[at, :])

    def listed(which, group, b):
        count = ids_s[which, 4, group]
        hits = jnp.int32(0)
        for j in range(cap):
            hits = hits + ((ids_s[which, group, j] == b) & (j < count)).astype(jnp.int32)
        return hits

    mine = [listed(0, prv, b) for b in range(blocks)]
    theirs = [listed(1, g, b) for b in range(blocks)]
    live = [jnp.where(j < ids_s[1, 4, nxt], 0.0, NEG) for j in range(cap)]

    def own_with(first, last):
        for a in range(first, last):
            a_copies[a].wait_recv()
        s = dot_nt(own[...], prev[BLK * first : BLK * last, :])
        for a in range(first, last):
            at = slice(BLK * a, BLK * a + BLK)
            top = f_prev[:, at]
            for b in range(blocks):
                here = slice(BLK * b, BLK * b + BLK)
                x = s[here, BLK * (a - first) : BLK * (a - first) + BLK]
                x = x + jnp.where(mine[a] + theirs[b] > 0, 0.0, NEG)
                f_own[here, :] = jnp.maximum(f_own[here, :], x)
                top = jnp.maximum(top, tops(x))
            f_prev[:, at] = top

    def listed_with(first, last):
        s = dot_nt(lbuf[...], prev[BLK * first : BLK * last, :])
        for a in range(first, last):
            at = slice(BLK * a, BLK * a + BLK)
            top = f_prev[:, at]
            for j in range(cap):
                here = slice(BLK * j, BLK * j + BLK)
                x = s[here, BLK * (a - first) : BLK * (a - first) + BLK] + live[j]
                f_l[here, :] = jnp.maximum(f_l[here, :], x)
                top = jnp.maximum(top, tops(x))
            f_prev[:, at] = top

    for b in range(1, slots):
        if b == min(5, slots - 1):
            pl.when(late == 0)(functools.partial(own_with, 0, 1))
        shard(b)
    for k in range(1, slots):
        crow[k] = jnp.max(cacc[k], axis=0, keepdims=True)
    b_copies = [None] + [
        remote(crow.at[k], cret.at[k], b_send.at[k], b_recv.at[k], (g, to_owner[k])) for k in range(1, slots)
    ]
    pl.when(late == 1)(functools.partial(own_with, 0, 1))
    own_with(1, 4)
    for copy in l_copies:
        copy.wait_recv()
    listed_with(0, 4)
    own_with(4, blocks)
    listed_with(4, blocks)
    for j in range(cap):
        r2s[j] = jnp.max(rows_to_lanes(f_l[BLK * j : BLK * j + BLK, :]), axis=0, keepdims=True)
    f_row[...] = jnp.max(f_prev[...], axis=0, keepdims=True)
    r_copies = [
        remote(f_row, r1, r_send.at[0], r_recv.at[0], (prv, m)),
        remote(r2s, r2, r_send.at[1], r_recv.at[1], (nxt, m)),
    ]

    best = jnp.max(cacc[0], axis=0, keepdims=True)
    for k in range(1, slots):
        b_copies[k].wait_recv()
        best = jnp.maximum(best, cret[k])
    out[0:1, :] = best

    mine_best = [
        jnp.max(rows_to_lanes(f_own[BLK * b : BLK * b + BLK, :]), axis=0, keepdims=True) for b in range(blocks)
    ]
    for copy in r_copies:
        copy.wait_recv()
    for b in range(blocks):
        at = slice(BLK * b, BLK * b + BLK)
        x = jnp.maximum(mine_best[b], r1[:, at])
        for j in range(cap):
            x = jnp.maximum(x, r2[j] + jnp.where(ids_s[2, g, j] == b, 0.0, NEG))
        out[1:2, at] = x

    for copy in id_copies + c_copies[1:] + a_copies + l_copies + b_copies[1:] + r_copies:
        copy.wait_send()


def solution(mesh):
    groups, members = mesh.shape["grp"], mesh.shape["mem"]
    cover = COVERS[members]
    slots = len(cover)

    def step(bank, pattern, pair_list, pair_count):
        rows, width = bank.shape
        blocks, group_blocks = pattern.shape
        cap = pair_list.shape[2]
        message = rows // 2 + 32
        bf16, f32, i32 = jnp.bfloat16, jnp.float32, jnp.int32
        vmem = pl.BlockSpec(memory_space=pltpu.VMEM)
        dma = pltpu.SemaphoreType.DMA
        out = pl.pallas_call(
            functools.partial(kernel, cover, groups, members),
            out_shape=jax.ShapeDtypeStruct((2, rows), f32),
            in_specs=[pl.BlockSpec(memory_space=pltpu.HBM)] * 4,
            out_specs=vmem,
            scratch_shapes=[
                pltpu.VMEM(pattern.shape, i32),
                pltpu.VMEM(pair_list.shape, i32),
                pltpu.VMEM(pair_count.shape, i32),
                pltpu.VMEM((rows, width), bf16),
                pltpu.VMEM((rows, 128), bf16),
                pltpu.VMEM((rows, width), bf16),
                pltpu.VMEM((cap * BLK, width), bf16),
                pltpu.VMEM((cap * BLK, width), bf16),
                pltpu.VMEM((slots, message, 128), bf16),
                pltpu.VMEM((slots, rows, 128), bf16),
                pltpu.VMEM((slots, rows, 128), bf16),
                pltpu.VMEM((rows, 128), f32),
                pltpu.VMEM((slots, 8, rows), f32),
                pltpu.VMEM((slots, 1, rows), f32),
                pltpu.VMEM((slots, 1, rows), f32),
                pltpu.VMEM((32, 128), i32),
                pltpu.VMEM((384, 128), bf16),
                pltpu.VMEM((3, 8, 128), i32),
                pltpu.SMEM((3, 8, 128), i32),
                pltpu.VMEM((rows, 128), f32),
                pltpu.VMEM((8, rows), f32),
                pltpu.VMEM((1, rows), f32),
                pltpu.VMEM((cap * BLK, 128), f32),
                pltpu.VMEM((cap, 1, 128), f32),
                pltpu.VMEM((1, rows), f32),
                pltpu.VMEM((cap, 1, 128), f32),
                dma((6,)),
                dma((2,)), dma((2,)),
                dma((slots,)), dma((slots,)),
                dma((blocks,)), dma((blocks,)),
                dma((cap,)), dma((cap,)),
                dma((slots,)), dma((slots,)),
                dma((2,)), dma((2,)),
                pltpu.SemaphoreType.REGULAR,
                pltpu.SemaphoreType.REGULAR,
            ],
            compiler_params=pltpu.CompilerParams(
                collective_id=0, has_side_effects=True, vmem_limit_bytes=60 * 1024 * 1024
            ),
            name="pair_search",
        )(bank, pattern, pair_list, pair_count)
        return out[0], out[1]

    return jax.shard_map(
        step,
        mesh=mesh,
        in_specs=(
            P(("grp", "mem"), None),
            P(("grp", "mem"), None),
            P(("grp", "mem"), None, None),
            P(("grp", "mem"), None),
        ),
        out_specs=(P(("grp", "mem")), P(("grp", "mem"))),
        check_vma=False,
    )
```

```python
import functools

import jax
import jax.numpy as jnp
from jax import lax
from jax.experimental import pallas as pl
from jax.experimental.pallas import tpu as pltpu
from jax.sharding import PartitionSpec as P

PREF = 64
BLK = 128
NEG = -1e30
MESH = pl.DeviceIdType.MESH
COVERS = {64: (0, 1, 2, 16, 5, 14, 34, 59, 42), 4: (0, 1, 2)}


def dot_nt(a, b):
    return lax.dot_general(a, b, (((1,), (1,)), ((), ())), preferred_element_type=jnp.float32)


def shifted(m, d, members):
    if members != 64:
        return lax.rem(m + d, members)
    at = lax.rem(((m // 2) % 4) * 16 + (m // 8) * 2 + m % 2 + d, members)
    return ((at // 2) % 8) * 8 + (at // 16) * 2 + at % 2


def kernel(
    cover, groups, members,
    bank, patt_in, plist_in, pcount_in,
    out,
    patt, plist, pcount, own, pre, prev, lbuf, lsend, recv, lhs, rhs, racc, cacc, crow, cret,
    pattpad, sel, ids, ids_s, f_own, f_prev, f_row, f_l, r2s, r1, r2,
    loc_sem, id_send, id_recv, c_send, c_recv, a_send, a_recv, l_send, l_recv, b_send, b_recv, r_send, r_recv, go_sem, mem_sem,
):
    g = lax.axis_index("grp")
    m = lax.axis_index("mem")
    core = lax.rem(m, 2)
    nxt = lax.rem(g + 1 + 2 * core, groups)
    prv = lax.rem(g + 3 - 2 * core, groups)
    opp = lax.rem(g + 2, groups)
    slots = len(cover)
    rows = own.shape[0]
    half = rows // 2
    blocks = rows // BLK
    cap = lbuf.shape[0] // BLK
    to_user = [None] + [shifted(m, members - d, members) for d in cover[1:]]
    to_owner = [None] + [shifted(m, d, members) for d in cover[1:]]

    pre_copy = pltpu.make_async_copy(bank.at[:, pl.ds(0, 128)], pre, loc_sem.at[0])
    pre_copy.start()
    small_copies = [
        pltpu.make_async_copy(src, dst, loc_sem.at[at])
        for src, dst, at in ((plist_in, plist, 3), (pcount_in, pcount, 4), (patt_in, patt, 5))
    ]
    for copy in small_copies:
        copy.start()
    own_copy = pltpu.make_async_copy(bank, own, loc_sem.at[1])
    own_copy.start()

    barrier = pltpu.get_barrier_semaphore()
    for step in range(1, groups):
        other = lax.rem(g + step, groups)

        @pl.when(other != 0)
        def _():
            pl.semaphore_signal(barrier, inc=1, device_id=(other, m), device_id_type=MESH)

    @pl.when(g != 0)
    def _():
        pl.semaphore_wait(barrier, groups - 1)

    @pl.when(g == 1)
    def _():
        pl.semaphore_signal(go_sem, inc=1, device_id=(0, m), device_id_type=MESH)

    @pl.when(g == 1)
    def _():
        for k in range(1, slots):
            for other in (to_user[k], to_owner[k]):
                pl.semaphore_signal(barrier, inc=1, device_id=(0, other), device_id_type=MESH)

    @pl.when(g == 0)
    def _():
        pl.semaphore_wait(go_sem, 1)

    def planned(src, dst, send, rcv, where):
        return pltpu.make_async_remote_copy(
            src_ref=src, dst_ref=dst, send_sem=send, recv_sem=rcv, device_id=where, device_id_type=MESH
        )

    def remote(*args):
        copy = planned(*args)
        copy.start()
        return copy

    ids[0] = jnp.zeros((8, 128), jnp.int32)
    pattpad[...] = jnp.zeros_like(pattpad)
    for copy in small_copies:
        copy.wait()
    ids[0, 0:4, 0:4] = plist[0]
    ids[0, 4:5, 0:4] = pcount[...]
    id_copies = [
        remote(ids.at[0], ids.at[1], id_send.at[0], id_recv.at[0], (nxt, m)),
        remote(ids.at[0], ids.at[2], id_send.at[1], id_recv.at[1], (opp, m)),
    ]
    a_copies = []
    for a in range(blocks):
        part = pl.ds(BLK * a, BLK)
        a_copies.append(remote(bank.at[part, :], prev.at[part, :], a_send.at[a], a_recv.at[a], (nxt, m)))

    lane = lax.broadcasted_iota(jnp.int32, (1, 128), 1)
    low = (lane < PREF).astype(jnp.float32)

    for t in range(3):
        pattpad[8 * t : 8 * t + blocks, :] = patt[:, 128 * t : 128 * t + 128]
    recv[0, half : half + 32, :] = pattpad[...].astype(jnp.float32).astype(jnp.bfloat16)
    pre_copy.wait()
    recv[0, 0:half, :] = (
        pre[0:half, :].astype(jnp.float32) * low
        + pltpu.roll(pre[half:rows, :].astype(jnp.float32) * low, PREF, 1)
    ).astype(jnp.bfloat16)

    c_copies = [None] + [
        planned(recv.at[0], recv.at[k], c_send.at[k], c_recv.at[k], (g, to_user[k])) for k in range(1, slots)
    ]

    def send_prefixes():
        @pl.when(g == 0)
        def _():
            pl.semaphore_wait(barrier, 2 * (slots - 1))
            for other in range(1, groups):
                pl.semaphore_signal(mem_sem, inc=1, device_id=(other, m), device_id_type=MESH)

        @pl.when(g != 0)
        def _():
            pl.semaphore_wait(mem_sem, 1)

        for copy in c_copies[1:]:
            copy.start()

    late = m // (members // 2)
    pl.when(late == 1)(send_prefixes)

    own_copy.wait()
    for copy in id_copies:
        copy.wait_recv()
    id_local = pltpu.make_async_copy(ids, ids_s, loc_sem.at[2])
    id_local.start()
    id_local.wait()
    l_copies = []
    for j in range(cap):
        block = ids_s[2, g, j]
        picked = own[0:BLK, :]
        for b in range(1, blocks):
            picked = lax.select(block == b, own[BLK * b : BLK * b + BLK, :], picked)
        lsend[BLK * j : BLK * j + BLK, :] = picked
        part = pl.ds(BLK * j, BLK)
        l_copies.append(remote(lsend.at[part, :], lbuf.at[part, :], l_send.at[j], l_recv.at[j], (prv, m)))

    pl.when(late == 0)(send_prefixes)

    column = jnp.full((1, 128), -1, jnp.int32)
    for k in range(slots):
        first = PREF + blocks * k
        member = m if k == 0 else to_owner[k]
        column = jnp.where((lane >= first) & (lane < first + blocks), blocks * member + lane - first, column)
    row_id = lax.broadcasted_iota(jnp.int32, sel.shape, 0)
    sel[...] = (row_id == column).astype(jnp.float32).astype(jnp.bfloat16)
    in_mask = ((lane >= PREF) & (lane < PREF + blocks * slots)).astype(jnp.float32)

    def build(k):
        parts = [
            jnp.dot(
                recv[k, half + 16 * (t // 2) : half + 16 * (t // 2) + 16, :],
                sel[128 * t : 128 * t + 128, :],
                preferred_element_type=jnp.float32,
            )
            for t in range(3)
        ]
        bias = parts[0][0:8] + parts[1][8:16] + parts[2][0:8]
        bias = (bias - 1.0) * (-NEG) * in_mask
        for b in range(blocks):
            at = BLK * (b % (blocks // 2))
            part = recv[k, at : at + BLK, :].astype(jnp.float32)
            if b >= blocks // 2:
                part = pltpu.roll(part, PREF, 1)
            part = part * low
            hot = (lane == PREF + blocks * k + b).astype(jnp.float32)
            lhs[k, BLK * b : BLK * b + BLK, :] = (part + hot).astype(jnp.bfloat16)
            rhs[k, BLK * b : BLK * b + BLK, :] = (part + bias[b : b + 1, :]).astype(jnp.bfloat16)

    f_own[...] = jnp.full_like(f_own, NEG)
    f_prev[...] = jnp.full_like(f_prev, NEG)
    f_l[...] = jnp.full_like(f_l, NEG)

    def tops(x):
        return jnp.max(x.reshape(BLK // 8, 8, BLK), axis=0)

    def rows_to_lanes(x):
        return jnp.max(x.T.reshape(16, 8, 128), axis=0)

    build(0)
    diag = jnp.where(
        lax.broadcasted_iota(jnp.int32, (BLK, BLK), 0) == lax.broadcasted_iota(jnp.int32, (BLK, BLK), 1), NEG, 0.0
    )
    for c in range(blocks):
        part = slice(BLK * c, BLK * c + BLK)
        s = dot_nt(lhs[0], rhs[0, part, :])
        top = jnp.full((8, BLK), NEG, jnp.float32)
        for b in range(blocks):
            x = s[BLK * b : BLK * b + BLK, :]
            if b == c:
                x = x + diag
            top = jnp.maximum(top, tops(x))
        cacc[0, :, part] = top

    done = set()

    def shard(b):
        c_copies[b].wait_recv()
        build(b)
        racc[...] = jnp.full_like(racc, NEG)
        for a in range(b):
            gap = (cover[a] - cover[b]) % members
            if min(gap, members - gap) in done:
                continue
            done.add(min(gap, members - gap))
            for n in range(0, rows, 256):
                s = dot_nt(lhs[b], rhs[a, n : n + 256, :])
                racc[...] = jnp.maximum(racc[...], jnp.maximum(s[:, 0:128], s[:, 128:256]))
                cacc[a, :, n : n + 256] = jnp.maximum(
                    cacc[a, :, n : n + 256], jnp.max(s.reshape(rows // 8, 8, 256), axis=0)
                )
        for c in range(blocks):
            at = slice(BLK * c, BLK * c + BLK)
            cacc[b, :, at] = rows_to_lanes(racc[at, :])

    def listed(which, group, b):
        count = ids_s[which, 4, group]
        hits = jnp.int32(0)
        for j in range(cap):
            hits = hits + ((ids_s[which, group, j] == b) & (j < count)).astype(jnp.int32)
        return hits

    mine = [listed(0, prv, b) for b in range(blocks)]
    theirs = [listed(1, g, b) for b in range(blocks)]
    live = [jnp.where(j < ids_s[1, 4, nxt], 0.0, NEG) for j in range(cap)]

    def own_with(first, last):
        for a in range(first, last):
            a_copies[a].wait_recv()
        s = dot_nt(own[...], prev[BLK * first : BLK * last, :])
        for a in range(first, last):
            at = slice(BLK * a, BLK * a + BLK)
            top = f_prev[:, at]
            for b in range(blocks):
                here = slice(BLK * b, BLK * b + BLK)
                x = s[here, BLK * (a - first) : BLK * (a - first) + BLK]
                x = x + jnp.where(mine[a] + theirs[b] > 0, 0.0, NEG)
                f_own[here, :] = jnp.maximum(f_own[here, :], x)
                top = jnp.maximum(top, tops(x))
            f_prev[:, at] = top

    def listed_with(first, last):
        s = dot_nt(lbuf[...], prev[BLK * first : BLK * last, :])
        for a in range(first, last):
            at = slice(BLK * a, BLK * a + BLK)
            top = f_prev[:, at]
            for j in range(cap):
                here = slice(BLK * j, BLK * j + BLK)
                x = s[here, BLK * (a - first) : BLK * (a - first) + BLK] + live[j]
                f_l[here, :] = jnp.maximum(f_l[here, :], x)
                top = jnp.maximum(top, tops(x))
            f_prev[:, at] = top

    for b in range(1, slots):
        if b == min(5, slots - 1):
            pl.when(late == 0)(functools.partial(own_with, 0, 1))
        shard(b)
    for k in range(1, slots):
        crow[k] = jnp.max(cacc[k], axis=0, keepdims=True)
    b_copies = [None] + [
        remote(crow.at[k], cret.at[k], b_send.at[k], b_recv.at[k], (g, to_owner[k])) for k in range(1, slots)
    ]
    pl.when(late == 1)(functools.partial(own_with, 0, 1))
    own_with(1, 4)
    for copy in l_copies:
        copy.wait_recv()
    listed_with(0, 4)
    own_with(4, blocks)
    listed_with(4, blocks)
    for j in range(cap):
        r2s[j] = jnp.max(rows_to_lanes(f_l[BLK * j : BLK * j + BLK, :]), axis=0, keepdims=True)
    f_row[...] = jnp.max(f_prev[...], axis=0, keepdims=True)
    r_copies = [
        remote(f_row, r1, r_send.at[0], r_recv.at[0], (prv, m)),
        remote(r2s, r2, r_send.at[1], r_recv.at[1], (nxt, m)),
    ]

    best = jnp.max(cacc[0], axis=0, keepdims=True)
    for k in range(1, slots):
        b_copies[k].wait_recv()
        best = jnp.maximum(best, cret[k])
    out[0:1, :] = best

    mine_best = [
        jnp.max(rows_to_lanes(f_own[BLK * b : BLK * b + BLK, :]), axis=0, keepdims=True) for b in range(blocks)
    ]
    for copy in r_copies:
        copy.wait_recv()
    for b in range(blocks):
        at = slice(BLK * b, BLK * b + BLK)
        x = jnp.maximum(mine_best[b], r1[:, at])
        for j in range(cap):
            x = jnp.maximum(x, r2[j] + jnp.where(ids_s[2, g, j] == b, 0.0, NEG))
        out[1:2, at] = x

    for copy in id_copies + c_copies[1:] + a_copies + l_copies + b_copies[1:] + r_copies:
        copy.wait_send()


def solution(mesh):
    groups, members = mesh.shape["grp"], mesh.shape["mem"]
    cover = COVERS[members]
    slots = len(cover)

    def step(bank, pattern, pair_list, pair_count):
        rows, width = bank.shape
        blocks, group_blocks = pattern.shape
        cap = pair_list.shape[2]
        message = rows // 2 + 32
        bf16, f32, i32 = jnp.bfloat16, jnp.float32, jnp.int32
        vmem = pl.BlockSpec(memory_space=pltpu.VMEM)
        dma = pltpu.SemaphoreType.DMA
        out = pl.pallas_call(
            functools.partial(kernel, cover, groups, members),
            out_shape=jax.ShapeDtypeStruct((2, rows), f32),
            in_specs=[pl.BlockSpec(memory_space=pltpu.HBM)] * 4,
            out_specs=vmem,
            scratch_shapes=[
                pltpu.VMEM(pattern.shape, i32),
                pltpu.VMEM(pair_list.shape, i32),
                pltpu.VMEM(pair_count.shape, i32),
                pltpu.VMEM((rows, width), bf16),
                pltpu.VMEM((rows, 128), bf16),
                pltpu.VMEM((rows, width), bf16),
                pltpu.VMEM((cap * BLK, width), bf16),
                pltpu.VMEM((cap * BLK, width), bf16),
                pltpu.VMEM((slots, message, 128), bf16),
                pltpu.VMEM((slots, rows, 128), bf16),
                pltpu.VMEM((slots, rows, 128), bf16),
                pltpu.VMEM((rows, 128), f32),
                pltpu.VMEM((slots, 8, rows), f32),
                pltpu.VMEM((slots, 1, rows), f32),
                pltpu.VMEM((slots, 1, rows), f32),
                pltpu.VMEM((32, 128), i32),
                pltpu.VMEM((384, 128), bf16),
                pltpu.VMEM((3, 8, 128), i32),
                pltpu.SMEM((3, 8, 128), i32),
                pltpu.VMEM((rows, 128), f32),
                pltpu.VMEM((8, rows), f32),
                pltpu.VMEM((1, rows), f32),
                pltpu.VMEM((cap * BLK, 128), f32),
                pltpu.VMEM((cap, 1, 128), f32),
                pltpu.VMEM((1, rows), f32),
                pltpu.VMEM((cap, 1, 128), f32),
                dma((6,)),
                dma((2,)), dma((2,)),
                dma((slots,)), dma((slots,)),
                dma((blocks,)), dma((blocks,)),
                dma((cap,)), dma((cap,)),
                dma((slots,)), dma((slots,)),
                dma((2,)), dma((2,)),
                pltpu.SemaphoreType.REGULAR,
                pltpu.SemaphoreType.REGULAR,
            ],
            compiler_params=pltpu.CompilerParams(
                collective_id=0, has_side_effects=True, vmem_limit_bytes=60 * 1024 * 1024
            ),
            name="pair_search",
        )(bank, pattern, pair_list, pair_count)
        return out[0], out[1]

    return jax.shard_map(
        step,
        mesh=mesh,
        in_specs=(
            P(("grp", "mem"), None),
            P(("grp", "mem"), None),
            P(("grp", "mem"), None, None),
            P(("grp", "mem"), None),
        ),
        out_specs=(P(("grp", "mem")), P(("grp", "mem"))),
        check_vma=False,
    )
```
